32 devices in a mesh: sample: 2 (over y), gx: 16 (over z, x, core).
Axes of the slice: x: 2, y: 2, z: 4, core: 2. Of those that a mesh axis runs over, the one named last changes fastest.
Arguments:
- populations: float32 [19, 32, 128, 256], P(None, ('sample', 'gx')), parts along dimension 1, may hold values from 0.5 to 1.5
- solid_mask: int32 [32, 128, 256], P(('sample', 'gx')), parts along dimension 0, may hold values from 0 to 1, as said below
- relax_rates: float32 [19], replicated, may hold values from 0.7 to 1.9
- body_force: float32 [3], replicated, may hold values from -0.1 to 0.1
Outputs:
- final_populations: float32 [19, 32, 128, 256], P(None, ('sample', 'gx')), parts along dimension 1
The draws below stay inside these ranges and needn't reach their ends.
There are 2 independent parts, one for each index of `sample`. The reference program is written for one: setup_inputs(seed, part) draws one part's arguments, and reference() takes and returns one part's arrays. A program takes and returns all parts, laid end to end along the dimension named above; an argument that names none is the same for every part. Nothing has to cross between parts.
Inputs may be any that keep to these rules, and one draw needn't show every extreme that they name: `solid_mask`: 1 marks a solid node, 0 a fluid node.
All inputs are finite; a program needn't handle non-finite values.
Results may differ from the reference program's by a relative error of at most 0.0003.
Values sent between devices are 32-bit elements; how exact they have to be, the bound alone decides.
A program may use at most 192 MiB of HBM per device.

```python
import jax
import jax.numpy as jnp
import numpy as np
from jax import lax

NY = 128
NZ = 256
STEPS = 2
NX = 16


def draw_solid_mask(key, part):
    position = lax.broadcasted_iota(jnp.int32, (NX, NY, NZ), 0)
    threshold = 50 + 550 * position // NX
    chance = jax.random.randint(jax.random.fold_in(key, 11), (NX, NY, NZ), 0, 1000)
    return (chance < threshold).astype(jnp.int32)


def levels(key, dims, pieces, smallest, largest):
    gain = 1.0
    for dim, parts in pieces:
        heights = jax.random.uniform(jax.random.fold_in(jax.random.fold_in(key, 6), dim), (parts,), jnp.float32, smallest / len(pieces), largest / len(pieces))
        gain = gain * jnp.repeat(jnp.exp(heights), dims[dim] // parts).reshape((-1,) + (1,) * (len(dims) - 1 - dim))
    return gain


def setup_inputs(seed: int = 0, part: int = 0) -> dict:
    key_of = jax.random.split(jax.random.key(seed), 5)
    part_keys = jax.random.split(jax.random.fold_in(key_of[4], part), 5)
    populations = jnp.clip(0.5 + 1.0 * jax.random.uniform(part_keys[0], (19, NX, NY, NZ), jnp.float32) ** levels(part_keys[0], (19, NX, NY, NZ), ((1, 16),), -0.2, 0.2), 0.5, 1.5)
    solid_mask = draw_solid_mask(jax.random.fold_in(jax.random.fold_in(key_of[4], part), 71), part)
    relax_rates = jnp.clip(jax.random.uniform(key_of[2], (19,), jnp.float32, 0.7, 1.9), 0.7, 1.9)
    body_force = jnp.clip(jax.random.uniform(key_of[3], (3,), jnp.float32, -0.1, 0.1), -0.1, 0.1)
    return {"populations": populations, "solid_mask": solid_mask, "relax_rates": relax_rates, "body_force": body_force}


def lattice_tables():
    velocities = np.array([[0, 0, 0], [1, 0, 0], [-1, 0, 0], [0, 1, 0], [0, -1, 0], [0, 0, 1], [0, 0, -1], [1, 1, 0], [-1, -1, 0], [1, -1, 0], [-1, 1, 0], [1, 0, 1], [-1, 0, -1], [1, 0, -1], [-1, 0, 1], [0, 1, 1], [0, -1, -1], [0, 1, -1], [0, -1, 1]])
    opposite = np.array([0, 2, 1, 4, 3, 6, 5, 8, 7, 10, 9, 12, 11, 14, 13, 16, 15, 18, 17])
    weights = np.array([1.0 / 3.0] + [1.0 / 18.0] * 6 + [1.0 / 36.0] * 12)
    along_x = velocities[:, 0]
    along_y = velocities[:, 1]
    along_z = velocities[:, 2]
    unity = np.ones(19)
    polynomials = np.stack([unity, along_x, along_y, along_z, along_x * along_y, along_x * along_z, along_y * along_z, along_x ** 2, along_y ** 2, along_z ** 2, along_x * along_y ** 2, along_x * along_z ** 2, along_x ** 2 * along_y, along_x ** 2 * along_z, along_y * along_z ** 2, along_y ** 2 * along_z, along_x ** 2 * along_y ** 2, along_x ** 2 * along_z ** 2, along_y ** 2 * along_z ** 2])
    basis = []
    for moment_row in polynomials:
        vector = moment_row.copy()
        for earlier in basis:
            vector = vector - (vector @ earlier) / (earlier @ earlier) * earlier
        basis.append(vector)
    moments = np.stack(basis)
    inverse = moments.T / np.sum(moments ** 2, axis=1)[None, :]
    return velocities, opposite, weights, moments, inverse


def make_kernel(relax_rates, tables):
    inverse = jnp.asarray(tables[4], jnp.float32)
    moments = jnp.asarray(tables[3], jnp.float32)
    return jnp.dot(inverse * relax_rates[None, :], moments, precision=lax.Precision.HIGHEST)


def collide(populations, solid_mask, kernel, body_force, tables):
    lattice_vel = jnp.asarray(tables[0], jnp.float32)
    weight_col = jnp.asarray(tables[2], jnp.float32)[:, None]
    density = jnp.sum(populations, axis=0)
    momentum = jnp.dot(lattice_vel.T, populations, precision=lax.Precision.HIGHEST)
    velocity = momentum / density
    projected = jnp.dot(lattice_vel, velocity, precision=lax.Precision.HIGHEST)
    speed_sq = jnp.sum(velocity * velocity, axis=0)
    equilibrium = weight_col * density * (1.0 + 3.0 * projected + 4.5 * projected * projected - 1.5 * speed_sq)
    relaxed = populations - jnp.dot(kernel, populations - equilibrium, precision=lax.Precision.HIGHEST)
    pushed = 3.0 * jnp.dot(lattice_vel, body_force, precision=lax.Precision.HIGHEST)
    relaxed = relaxed + (weight_col * pushed[:, None]) * density
    reflected = populations[tables[1]]
    return jnp.where(solid_mask[None, :] == 1, reflected, relaxed)


def reference(populations, solid_mask, relax_rates, body_force):
    tables = lattice_tables()
    kernel = make_kernel(relax_rates, tables)
    state = populations

    def one_plane(pair):
        plane, mask_plane = pair
        flat = collide(plane.reshape(19, -1), mask_plane.reshape(-1), kernel, body_force, tables)
        return flat.reshape(plane.shape)

    for step in range(STEPS):
        planes = jnp.moveaxis(state, 1, 0)
        relaxed = jnp.moveaxis(lax.map(one_plane, (planes, solid_mask)), 0, 1)
        moved = []
        for number in range(19):
            offsets = tuple(int(value) for value in tables[0][number])
            moved.append(jnp.roll(relaxed[number], offsets, axis=(0, 1, 2)))
        state = jnp.stack(moved)
    return state
```

```python
import jax
import jax.numpy as jnp
import numpy as np
from jax import lax
from jax.experimental import pallas as pl
from jax.experimental.pallas import tpu as pltpu
from jax.sharding import PartitionSpec as P

CHUNK_ROWS = 16
GROUP_ROWS = 8

VELOCITIES = [
    (0, 0, 0), (1, 0, 0), (-1, 0, 0), (0, 1, 0), (0, -1, 0), (0, 0, 1), (0, 0, -1),
    (1, 1, 0), (-1, -1, 0), (1, -1, 0), (-1, 1, 0), (1, 0, 1), (-1, 0, -1), (1, 0, -1),
    (-1, 0, 1), (0, 1, 1), (0, -1, -1), (0, 1, -1), (0, -1, 1),
]
OPPOSITE = [0, 2, 1, 4, 3, 6, 5, 8, 7, 10, 9, 12, 11, 14, 13, 16, 15, 18, 17]
LEVEL = [i for i in range(19) if VELOCITIES[i][0] == 0]
RISING = [i for i in range(19) if VELOCITIES[i][0] == 1]
FALLING = [i for i in range(19) if VELOCITIES[i][0] == -1]

EVEN_ROWS, EVEN_CLASS = (0, 7, 8, 9, 16, 17, 18), (0, 1, 3, 5, 7, 11, 15)
CROSS_ROWS = (4, 5, 6)
ODD_ROWS = ((1, 10, 11), (2, 12, 14), (3, 13, 15))
ODD_CLASS = ((1, 7, 11), (3, 7, 15), (5, 11, 15))


def moment_rows():
    c = np.array(VELOCITIES, np.float64)
    x, y, z = c[:, 0], c[:, 1], c[:, 2]
    polynomials = [
        np.ones(19), x, y, z, x * y, x * z, y * z, x**2, y**2, z**2, x * y**2, x * z**2,
        x**2 * y, x**2 * z, y * z**2, y**2 * z, x**2 * y**2, x**2 * z**2, y**2 * z**2,
    ]
    basis = []
    for row in polynomials:
        vector = row.copy()
        for earlier in basis:
            vector = vector - (vector @ earlier) / (earlier @ earlier) * earlier
        basis.append(vector)
    moments = np.stack(basis)
    return moments, np.sum(moments**2, axis=1)


MOMENTS, NORMS = moment_rows()


def kernel_entries():
    entries = {}
    for a in range(7):
        for b in range(a, 7):
            entries["even", a, b] = [
                (r, MOMENTS[r, EVEN_CLASS[a]] * MOMENTS[r, EVEN_CLASS[b]] / NORMS[r])
                for r in EVEN_ROWS
            ]
    for axis in range(3):
        for a in range(3):
            for b in range(a, 3):
                entries["odd", axis, a, b] = [
                    (
                        r,
                        MOMENTS[r, ODD_CLASS[axis][a]] * MOMENTS[r, ODD_CLASS[axis][b]] / NORMS[r],
                    )
                    for r in ODD_ROWS[axis]
                ]
    for k in range(3):
        entries["cross", k] = [(CROSS_ROWS[k], 1.0 / NORMS[CROSS_ROWS[k]])]
    return entries


ENTRIES = kernel_entries()
PLACE = {name: number for number, name in enumerate(ENTRIES)}


def fill_table(table, rates_ref):
    for name, terms in ENTRIES.items():
        total = None
        for r, factor in terms:
            if abs(factor) < 1e-12:
                continue
            term = rates_ref[r] * np.float32(factor)
            total = term if total is None else total + term
        table[PLACE[name]] = total if total is not None else jnp.float32(0.0)


def collide(f, solid, table, force):
    def even(a, b):
        return table[PLACE["even", min(a, b), max(a, b)]]

    def odd(axis, a, b):
        return table[PLACE["odd", axis, min(a, b), max(a, b)]]

    p = {i: f[i] + f[i + 1] for i in range(1, 19, 2)}
    d = {i: f[i] - f[i + 1] for i in range(1, 19, 2)}
    q_xy, q_xz, q_yz = p[7] + p[9], p[11] + p[13], p[15] + p[17]
    rho = f[0] + (p[1] + p[3] + p[5]) + (q_xy + q_xz + q_yz)
    x_parts = [d[1], d[7] + d[9], d[11] + d[13]]
    y_parts = [d[3], d[7] - d[9], d[15] + d[17]]
    z_parts = [d[5], d[11] - d[13], d[15] - d[17]]
    parts = [x_parts, y_parts, z_parts]
    j = [v[0] + v[1] + v[2] for v in parts]
    inverse = 1.0 / rho
    u = [v * inverse for v in j]
    xx, yy, zz = j[0] * u[0], j[1] * u[1], j[2] * u[2]
    square = xx + yy + zz
    third = 1.0 / 3.0
    base = rho * (1.0 / 9.0) - square * (1.0 / 6.0)
    e = [
        f[0] - (rho * third - 0.5 * square),
        p[1] - (base + 0.5 * xx),
        p[3] - (base + 0.5 * yy),
        p[5] - (base + 0.5 * zz),
        q_xy - (base + 0.5 * (xx + yy)),
        q_xz - (base + 0.5 * (xx + zz)),
        q_yz - (base + 0.5 * (yy + zz)),
    ]
    cross = [
        table[PLACE["cross", 0]] * ((p[7] - p[9]) - j[0] * u[1]),
        table[PLACE["cross", 1]] * ((p[11] - p[13]) - j[0] * u[2]),
        table[PLACE["cross", 2]] * ((p[15] - p[17]) - j[1] * u[2]),
    ]
    even_out = []
    for a in range(7):
        total = even(a, 0) * e[0]
        for b in range(1, 7):
            total = total + even(a, b) * e[b]
        even_out.append(total)
    odd_out = []
    for axis in range(3):
        share = j[axis] * third
        n = [v - share for v in parts[axis]]
        out = []
        for a in range(3):
            total = odd(axis, a, 0) * n[0] + odd(axis, a, 1) * n[1] + odd(axis, a, 2) * n[2]
            push = force[axis] * np.float32(1.0 / 6.0 if a == 0 else 1.0 / 12.0)
            out.append(push * rho - total)
        odd_out.append(out)
    (x1, x_xy, x_xz), (y1, y_xy, y_yz), (z1, z_xz, z_yz) = odd_out
    even_part = {
        1: even_out[1], 3: even_out[2], 5: even_out[3],
        7: even_out[4] + cross[0], 9: even_out[4] - cross[0],
        11: even_out[5] + cross[1], 13: even_out[5] - cross[1],
        15: even_out[6] + cross[2], 17: even_out[6] - cross[2],
    }
    odd_part = {
        1: x1, 3: y1, 5: z1, 7: x_xy + y_xy, 9: x_xy - y_xy,
        11: x_xz + z_xz, 13: x_xz - z_xz, 15: y_yz + z_yz, 17: y_yz - z_yz,
    }
    relaxed = [jnp.where(solid, f[0], f[0] - even_out[0])]
    for i in range(1, 19, 2):
        relaxed.append(jnp.where(solid, f[i + 1], (f[i] - even_part[i]) + odd_part[i]))
        relaxed.append(jnp.where(solid, f[i], (f[i + 1] - even_part[i]) - odd_part[i]))
    return relaxed


def slot(i, level, moving):
    if i in LEVEL:
        return level.at[LEVEL.index(i)]
    if i in RISING:
        return moving.at[0, RISING.index(i)]
    return moving.at[1, FALLING.index(i)]


def steps_kernel(
    pops_ref, mask_ref, rates_ref, force_ref, level_out, moving_out,
    pops, mask, level1, send1, recv1, level2, send2, table,
    pops_sem, mask_sem, send_sem, recv_sem, out_sem,
):
    count = lax.axis_size("gx")
    me = lax.axis_index("gx")
    targets = (lax.rem(me + 1, count), lax.rem(me + count - 1, count))
    height, breadth = mask.shape
    chunks = height // CHUNK_ROWS

    def rows(c):
        return pl.ds(pl.multiple_of(c * CHUNK_ROWS, CHUNK_ROWS), CHUNK_ROWS)

    def bring_pops(c):
        return pltpu.make_async_copy(
            pops_ref.at[:, rows(c), :], pops.at[:, rows(c), :], pops_sem.at[c]
        )

    bring_mask = pltpu.make_async_copy(mask_ref, mask, mask_sem)

    def ship(turn, way, c):
        source, target = (send1, recv1) if turn == 0 else (send2, moving_out)
        return pltpu.make_async_remote_copy(
            src_ref=source.at[way, :, rows(c), :],
            dst_ref=target.at[way, :, rows(c), :],
            send_sem=send_sem.at[turn, way, c],
            recv_sem=recv_sem.at[turn, way, c],
            device_id={"gx": targets[way]},
            device_id_type=pl.DeviceIdType.MESH,
        )

    def put_level(c):
        return pltpu.make_async_copy(
            level2.at[:, rows(c), :], level_out.at[:, rows(c), :], out_sem.at[c]
        )

    bring_pops(chunks - 1).start()
    bring_mask.start()

    @pl.loop(0, chunks - 1)
    def _(c):
        bring_pops(c).start()

    barrier = pltpu.get_barrier_semaphore()
    for target in targets:
        pl.semaphore_signal(
            barrier, inc=1, device_id={"gx": target}, device_id_type=pl.DeviceIdType.MESH
        )
    fill_table(table, rates_ref)
    force = [force_ref[axis] for axis in range(3)]

    row = lax.broadcasted_iota(jnp.int32, (GROUP_ROWS, breadth), 0)

    def work(c, load, level, moving):
        for part in range(CHUNK_ROWS // GROUP_ROWS):
            start = pl.multiple_of(c * CHUNK_ROWS + part * GROUP_ROWS, GROUP_ROWS)
            here = pl.ds(start, GROUP_ROWS)
            f = [load(i, here) for i in range(19)]
            relaxed = collide(f, mask[here, :] == 1, table, force)
            for i in range(19):
                _, along_y, along_z = VELOCITIES[i]
                value, plane = relaxed[i], slot(i, level, moving)
                if along_z:
                    value = pltpu.roll(value, along_z % breadth, 1)
                if not along_y:
                    plane[here, :] = value
                    continue
                value = pltpu.roll(value, along_y % GROUP_ROWS, 0)
                beyond = lax.rem(start + (height + along_y * GROUP_ROWS), height)
                beyond = pl.ds(pl.multiple_of(beyond, GROUP_ROWS), GROUP_ROWS)
                crosses = row == (0 if along_y == 1 else GROUP_ROWS - 1)
                pltpu.store(plane.at[here, :], value, mask=jnp.logical_not(crosses))
                pltpu.store(plane.at[beyond, :], value, mask=crosses)

    bring_mask.wait()

    @pl.loop(0, chunks)
    def _(t):
        c = lax.rem(t + (chunks - 1), chunks)
        bring_pops(c).wait()
        work(c, lambda i, here: pops[i, here, :], level1, send1)

        @pl.when(t == 1)
        def _():
            pl.semaphore_wait(barrier, 2)

        @pl.when(t >= 2)
        def _():
            for way in range(2):
                ship(0, way, t - 2).start()

    for c in (chunks - 2, chunks - 1):
        for way in range(2):
            ship(0, way, c).start()

    def arrived(i, here):
        if i in LEVEL:
            return level1[LEVEL.index(i), here, :]
        return slot(i, None, recv1)[here, :]

    @pl.loop(0, chunks)
    def _(c):
        for way in range(2):
            ship(0, way, c).wait_recv()
        work(c, arrived, level2, send2)

        @pl.when(c >= 2)
        def _():
            for way in range(2):
                ship(1, way, c - 1).start()
            put_level(c - 1).start()

    for c in (chunks - 1, 0):
        for way in range(2):
            ship(1, way, c).start()
        put_level(c).start()

    @pl.loop(0, chunks)
    def _(c):
        for way in range(2):
            ship(0, way, c).wait_send()
            ship(1, way, c).wait_send()
            ship(1, way, c).wait_recv()
        put_level(c).wait()


def place_kernel(level_ref, moving_ref, out_ref, sems):
    copies = [
        pltpu.make_async_copy(slot(i, level_ref, moving_ref), out_ref.at[i], sems.at[i])
        for i in range(19)
    ]
    for copy in copies:
        copy.start()
    for copy in copies:
        copy.wait()


def on_device(populations, solid_mask, relax_rates, body_force):
    channels, depth, height, breadth = populations.shape
    chunks = height // CHUNK_ROWS
    f32 = jnp.float32
    anywhere = pl.BlockSpec(memory_space=pl.ANY)
    in_hbm = pl.BlockSpec(memory_space=pltpu.HBM)
    scalars = pl.BlockSpec(memory_space=pltpu.SMEM)
    level, moving = pl.pallas_call(
        steps_kernel,
        out_shape=(
            jax.ShapeDtypeStruct((len(LEVEL), height, breadth), f32),
            jax.ShapeDtypeStruct((2, len(RISING), height, breadth), f32),
        ),
        in_specs=[in_hbm, in_hbm, scalars, scalars],
        out_specs=(anywhere, anywhere),
        scratch_shapes=[
            pltpu.VMEM((channels, height, breadth), f32),
            pltpu.VMEM((height, breadth), jnp.int32),
            pltpu.VMEM((len(LEVEL), height, breadth), f32),
            pltpu.VMEM((2, len(RISING), height, breadth), f32),
            pltpu.VMEM((2, len(RISING), height, breadth), f32),
            pltpu.VMEM((len(LEVEL), height, breadth), f32),
            pltpu.VMEM((2, len(RISING), height, breadth), f32),
            pltpu.SMEM((len(ENTRIES),), f32),
            pltpu.SemaphoreType.DMA((chunks,)),
            pltpu.SemaphoreType.DMA,
            pltpu.SemaphoreType.DMA((2, 2, chunks)),
            pltpu.SemaphoreType.DMA((2, 2, chunks)),
            pltpu.SemaphoreType.DMA((chunks,)),
        ],
        compiler_params=pltpu.CompilerParams(
            collective_id=0, has_side_effects=True, vmem_limit_bytes=32 * 1024 * 1024
        ),
    )(
        populations.reshape(channels, height, breadth),
        solid_mask.reshape(height, breadth),
        relax_rates,
        body_force,
    )
    placed = pl.pallas_call(
        place_kernel,
        out_shape=jax.ShapeDtypeStruct((channels, height, breadth), f32),
        in_specs=[anywhere, anywhere],
        out_specs=in_hbm,
        scratch_shapes=[pltpu.SemaphoreType.DMA((channels,))],
        compiler_params=pltpu.CompilerParams(vmem_limit_bytes=1024 * 1024),
    )(level, moving)
    return placed.reshape(populations.shape)


def solution(mesh):
    in_specs = (P(None, ("sample", "gx"), None, None), P(("sample", "gx"), None, None), P(), P())
    out_specs = P(None, ("sample", "gx"), None, None)
    return jax.shard_map(
        on_device, mesh=mesh, in_specs=in_specs, out_specs=out_specs, check_vma=False
    )
```

```python
import jax
import jax.numpy as jnp
import numpy as np
from jax import lax
from jax.experimental import pallas as pl
from jax.experimental.pallas import tpu as pltpu
from jax.sharding import PartitionSpec as P

CHUNK_ROWS = 16
GROUP_ROWS = 8

VELOCITIES = [
    (0, 0, 0), (1, 0, 0), (-1, 0, 0), (0, 1, 0), (0, -1, 0), (0, 0, 1), (0, 0, -1),
    (1, 1, 0), (-1, -1, 0), (1, -1, 0), (-1, 1, 0), (1, 0, 1), (-1, 0, -1), (1, 0, -1),
    (-1, 0, 1), (0, 1, 1), (0, -1, -1), (0, 1, -1), (0, -1, 1),
]
OPPOSITE = [0, 2, 1, 4, 3, 6, 5, 8, 7, 10, 9, 12, 11, 14, 13, 16, 15, 18, 17]
LEVEL = [i for i in range(19) if VELOCITIES[i][0] == 0]
RISING = [i for i in range(19) if VELOCITIES[i][0] == 1]
FALLING = [i for i in range(19) if VELOCITIES[i][0] == -1]

EVEN_ROWS, EVEN_CLASS = (0, 7, 8, 9, 16, 17, 18), (0, 1, 3, 5, 7, 11, 15)
CROSS_ROWS = (4, 5, 6)
ODD_ROWS = ((1, 10, 11), (2, 12, 14), (3, 13, 15))
ODD_CLASS = ((1, 7, 11), (3, 7, 15), (5, 11, 15))


def moment_rows():
    c = np.array(VELOCITIES, np.float64)
    x, y, z = c[:, 0], c[:, 1], c[:, 2]
    polynomials = [
        np.ones(19), x, y, z, x * y, x * z, y * z, x**2, y**2, z**2, x * y**2, x * z**2,
        x**2 * y, x**2 * z, y * z**2, y**2 * z, x**2 * y**2, x**2 * z**2, y**2 * z**2,
    ]
    basis = []
    for row in polynomials:
        vector = row.copy()
        for earlier in basis:
            vector = vector - (vector @ earlier) / (earlier @ earlier) * earlier
        basis.append(vector)
    moments = np.stack(basis)
    return moments, np.sum(moments**2, axis=1)


MOMENTS, NORMS = moment_rows()


def kernel_entries():
    entries = {}
    for a in range(7):
        for b in range(a, 7):
            entries["even", a, b] = [
                (r, MOMENTS[r, EVEN_CLASS[a]] * MOMENTS[r, EVEN_CLASS[b]] / NORMS[r])
                for r in EVEN_ROWS
            ]
    for axis in range(3):
        for a in range(3):
            for b in range(a, 3):
                entries["odd", axis, a, b] = [
                    (
                        r,
                        MOMENTS[r, ODD_CLASS[axis][a]] * MOMENTS[r, ODD_CLASS[axis][b]] / NORMS[r],
                    )
                    for r in ODD_ROWS[axis]
                ]
    for k in range(3):
        entries["cross", k] = [(CROSS_ROWS[k], 1.0 / NORMS[CROSS_ROWS[k]])]
    return entries


ENTRIES = kernel_entries()
PLACE = {name: number for number, name in enumerate(ENTRIES)}


def fill_table(table, rates_ref):
    for name, terms in ENTRIES.items():
        total = None
        for r, factor in terms:
            if abs(factor) < 1e-12:
                continue
            term = rates_ref[r] * np.float32(factor)
            total = term if total is None else total + term
        table[PLACE[name]] = total if total is not None else jnp.float32(0.0)


def collide(f, solid, table, force):
    def even(a, b):
        return table[PLACE["even", min(a, b), max(a, b)]]

    def odd(axis, a, b):
        return table[PLACE["odd", axis, min(a, b), max(a, b)]]

    p = {i: f[i] + f[i + 1] for i in range(1, 19, 2)}
    d = {i: f[i] - f[i + 1] for i in range(1, 19, 2)}
    q_xy, q_xz, q_yz = p[7] + p[9], p[11] + p[13], p[15] + p[17]
    rho = f[0] + (p[1] + p[3] + p[5]) + (q_xy + q_xz + q_yz)
    x_parts = [d[1], d[7] + d[9], d[11] + d[13]]
    y_parts = [d[3], d[7] - d[9], d[15] + d[17]]
    z_parts = [d[5], d[11] - d[13], d[15] - d[17]]
    parts = [x_parts, y_parts, z_parts]
    j = [v[0] + v[1] + v[2] for v in parts]
    inverse = 1.0 / rho
    u = [v * inverse for v in j]
    xx, yy, zz = j[0] * u[0], j[1] * u[1], j[2] * u[2]
    square = xx + yy + zz
    third = 1.0 / 3.0
    base = rho * (1.0 / 9.0) - square * (1.0 / 6.0)
    e = [
        f[0] - (rho * third - 0.5 * square),
        p[1] - (base + 0.5 * xx),
        p[3] - (base + 0.5 * yy),
        p[5] - (base + 0.5 * zz),
        q_xy - (base + 0.5 * (xx + yy)),
        q_xz - (base + 0.5 * (xx + zz)),
        q_yz - (base + 0.5 * (yy + zz)),
    ]
    cross = [
        table[PLACE["cross", 0]] * ((p[7] - p[9]) - j[0] * u[1]),
        table[PLACE["cross", 1]] * ((p[11] - p[13]) - j[0] * u[2]),
        table[PLACE["cross", 2]] * ((p[15] - p[17]) - j[1] * u[2]),
    ]
    even_out = []
    for a in range(7):
        total = even(a, 0) * e[0]
        for b in range(1, 7):
            total = total + even(a, b) * e[b]
        even_out.append(total)
    odd_out = []
    for axis in range(3):
        share = j[axis] * third
        n = [v - share for v in parts[axis]]
        out = []
        for a in range(3):
            total = odd(axis, a, 0) * n[0] + odd(axis, a, 1) * n[1] + odd(axis, a, 2) * n[2]
            push = force[axis] * np.float32(1.0 / 6.0 if a == 0 else 1.0 / 12.0)
            out.append(push * rho - total)
        odd_out.append(out)
    (x1, x_xy, x_xz), (y1, y_xy, y_yz), (z1, z_xz, z_yz) = odd_out
    even_part = {
        1: even_out[1], 3: even_out[2], 5: even_out[3],
        7: even_out[4] + cross[0], 9: even_out[4] - cross[0],
        11: even_out[5] + cross[1], 13: even_out[5] - cross[1],
        15: even_out[6] + cross[2], 17: even_out[6] - cross[2],
    }
    odd_part = {
        1: x1, 3: y1, 5: z1, 7: x_xy + y_xy, 9: x_xy - y_xy,
        11: x_xz + z_xz, 13: x_xz - z_xz, 15: y_yz + z_yz, 17: y_yz - z_yz,
    }
    relaxed = [jnp.where(solid, f[0], f[0] - even_out[0])]
    for i in range(1, 19, 2):
        relaxed.append(jnp.where(solid, f[i + 1], (f[i] - even_part[i]) + odd_part[i]))
        relaxed.append(jnp.where(solid, f[i], (f[i + 1] - even_part[i]) - odd_part[i]))
    return relaxed


def slot(i, level, moving):
    if i in LEVEL:
        return level.at[LEVEL.index(i)]
    if i in RISING:
        return moving.at[0, RISING.index(i)]
    return moving.at[1, FALLING.index(i)]


def steps_kernel(
    pops_ref, mask_ref, rates_hbm, force_hbm, level_out, moving_out,
    rates_ref, force_ref, pops, mask, level1, send1, recv1, level2, send2, table,
    scalar_sem, pops_sem, mask_sem, send_sem, recv_sem, out_sem,
):
    count = lax.axis_size("gx")
    me = lax.axis_index("gx")
    targets = (lax.rem(me + 1, count), lax.rem(me + count - 1, count))
    height, breadth = mask.shape
    chunks = height // CHUNK_ROWS

    def rows(c):
        return pl.ds(pl.multiple_of(c * CHUNK_ROWS, CHUNK_ROWS), CHUNK_ROWS)

    def bring_pops(c):
        return pltpu.make_async_copy(
            pops_ref.at[:, rows(c), :], pops.at[:, rows(c), :], pops_sem.at[c]
        )

    bring_mask = pltpu.make_async_copy(mask_ref, mask, mask_sem)

    def ship(turn, way, c):
        source, target = (send1, recv1) if turn == 0 else (send2, moving_out)
        return pltpu.make_async_remote_copy(
            src_ref=source.at[way, :, rows(c), :],
            dst_ref=target.at[way, :, rows(c), :],
            send_sem=send_sem.at[turn, way, c],
            recv_sem=recv_sem.at[turn, way, c],
            device_id={"gx": targets[way]},
            device_id_type=pl.DeviceIdType.MESH,
        )

    def put_level(c):
        return pltpu.make_async_copy(
            level2.at[:, rows(c), :], level_out.at[:, rows(c), :], out_sem.at[c]
        )

    bring_scalars = (
        pltpu.make_async_copy(rates_hbm, rates_ref, scalar_sem.at[0]),
        pltpu.make_async_copy(force_hbm, force_ref, scalar_sem.at[1]),
    )
    for bring in bring_scalars:
        bring.start()
    bring_pops(chunks - 1).start()
    bring_mask.start()

    @pl.loop(0, chunks - 1)
    def _(c):
        bring_pops(c).start()

    barrier = pltpu.get_barrier_semaphore()
    for target in targets:
        pl.semaphore_signal(
            barrier, inc=1, device_id={"gx": target}, device_id_type=pl.DeviceIdType.MESH
        )
    for bring in bring_scalars:
        bring.wait()
    fill_table(table, rates_ref)
    force = [force_ref[axis] for axis in range(3)]

    row = lax.broadcasted_iota(jnp.int32, (GROUP_ROWS, breadth), 0)

    def work(c, load, level, moving):
        for part in range(CHUNK_ROWS // GROUP_ROWS):
            start = pl.multiple_of(c * CHUNK_ROWS + part * GROUP_ROWS, GROUP_ROWS)
            here = pl.ds(start, GROUP_ROWS)
            f = [load(i, here) for i in range(19)]
            relaxed = collide(f, mask[here, :] == 1, table, force)
            for i in range(19):
                _, along_y, along_z = VELOCITIES[i]
                value, plane = relaxed[i], slot(i, level, moving)
                if along_z:
                    value = pltpu.roll(value, along_z % breadth, 1)
                if not along_y:
                    plane[here, :] = value
                    continue
                value = pltpu.roll(value, along_y % GROUP_ROWS, 0)
                beyond = lax.rem(start + (height + along_y * GROUP_ROWS), height)
                beyond = pl.ds(pl.multiple_of(beyond, GROUP_ROWS), GROUP_ROWS)
                crosses = row == (0 if along_y == 1 else GROUP_ROWS - 1)
                pltpu.store(plane.at[here, :], value, mask=jnp.logical_not(crosses))
                pltpu.store(plane.at[beyond, :], value, mask=crosses)

    bring_mask.wait()

    @pl.loop(0, chunks)
    def _(t):
        c = lax.rem(t + (chunks - 1), chunks)
        bring_pops(c).wait()
        work(c, lambda i, here: pops[i, here, :], level1, send1)

        @pl.when(t == 1)
        def _():
            pl.semaphore_wait(barrier, 2)

        @pl.when(t >= 2)
        def _():
            for way in range(2):
                ship(0, way, t - 2).start()

    for c in (chunks - 2, chunks - 1):
        for way in range(2):
            ship(0, way, c).start()

    def arrived(i, here):
        if i in LEVEL:
            return level1[LEVEL.index(i), here, :]
        return slot(i, None, recv1)[here, :]

    @pl.loop(0, chunks)
    def _(c):
        for way in range(2):
            ship(0, way, c).wait_recv()
        work(c, arrived, level2, send2)

        @pl.when(c >= 2)
        def _():
            for way in range(2):
                ship(1, way, c - 1).start()
            put_level(c - 1).start()

    for c in (chunks - 1, 0):
        for way in range(2):
            ship(1, way, c).start()
        put_level(c).start()

    @pl.loop(0, chunks)
    def _(c):
        for way in range(2):
            ship(0, way, c).wait_send()
            ship(1, way, c).wait_send()
            ship(1, way, c).wait_recv()
        put_level(c).wait()


def place_kernel(level_ref, moving_ref, out_ref, sems):
    copies = [
        pltpu.make_async_copy(slot(i, level_ref, moving_ref), out_ref.at[i], sems.at[i])
        for i in range(19)
    ]
    for copy in copies:
        copy.start()
    for copy in copies:
        copy.wait()


def on_device(populations, solid_mask, relax_rates, body_force):
    channels, depth, height, breadth = populations.shape
    chunks = height // CHUNK_ROWS
    f32 = jnp.float32
    anywhere = pl.BlockSpec(memory_space=pl.ANY)
    in_hbm = pl.BlockSpec(memory_space=pltpu.HBM)
    level, moving = pl.pallas_call(
        steps_kernel,
        out_shape=(
            jax.ShapeDtypeStruct((len(LEVEL), height, breadth), f32),
            jax.ShapeDtypeStruct((2, len(RISING), height, breadth), f32),
        ),
        in_specs=[in_hbm] * 4,
        out_specs=(anywhere, anywhere),
        scratch_shapes=[
            pltpu.SMEM(relax_rates.shape, f32),
            pltpu.SMEM(body_force.shape, f32),
            pltpu.VMEM((channels, height, breadth), f32),
            pltpu.VMEM((height, breadth), jnp.int32),
            pltpu.VMEM((len(LEVEL), height, breadth), f32),
            pltpu.VMEM((2, len(RISING), height, breadth), f32),
            pltpu.VMEM((2, len(RISING), height, breadth), f32),
            pltpu.VMEM((len(LEVEL), height, breadth), f32),
            pltpu.VMEM((2, len(RISING), height, breadth), f32),
            pltpu.SMEM((len(ENTRIES),), f32),
            pltpu.SemaphoreType.DMA((2,)),
            pltpu.SemaphoreType.DMA((chunks,)),
            pltpu.SemaphoreType.DMA,
            pltpu.SemaphoreType.DMA((2, 2, chunks)),
            pltpu.SemaphoreType.DMA((2, 2, chunks)),
            pltpu.SemaphoreType.DMA((chunks,)),
        ],
        compiler_params=pltpu.CompilerParams(
            collective_id=0, has_side_effects=True, vmem_limit_bytes=32 * 1024 * 1024
        ),
    )(
        pltpu.with_memory_space_constraint(populations.reshape(channels, height, breadth), pltpu.HBM),
        pltpu.with_memory_space_constraint(solid_mask.reshape(height, breadth), pltpu.HBM),
        pltpu.with_memory_space_constraint(relax_rates, pltpu.HBM),
        pltpu.with_memory_space_constraint(body_force, pltpu.HBM),
    )
    placed = pl.pallas_call(
        place_kernel,
        out_shape=jax.ShapeDtypeStruct((channels, height, breadth), f32),
        in_specs=[anywhere, anywhere],
        out_specs=in_hbm,
        scratch_shapes=[pltpu.SemaphoreType.DMA((channels,))],
        compiler_params=pltpu.CompilerParams(vmem_limit_bytes=1024 * 1024),
    )(level, moving)
    return placed.reshape(populations.shape)


def solution(mesh):
    in_specs = (P(None, ("sample", "gx"), None, None), P(("sample", "gx"), None, None), P(), P())
    out_specs = P(None, ("sample", "gx"), None, None)
    return jax.shard_map(
        on_device, mesh=mesh, in_specs=in_specs, out_specs=out_specs, check_vma=False
    )
```

```python
import jax
import jax.numpy as jnp
import numpy as np
from jax import lax
from jax.experimental import pallas as pl
from jax.experimental.pallas import tpu as pltpu
from jax.sharding import PartitionSpec as P

CHUNK_ROWS = 16
GROUP_ROWS = 8

VELOCITIES = [
    (0, 0, 0), (1, 0, 0), (-1, 0, 0), (0, 1, 0), (0, -1, 0), (0, 0, 1), (0, 0, -1),
    (1, 1, 0), (-1, -1, 0), (1, -1, 0), (-1, 1, 0), (1, 0, 1), (-1, 0, -1), (1, 0, -1),
    (-1, 0, 1), (0, 1, 1), (0, -1, -1), (0, 1, -1), (0, -1, 1),
]
OPPOSITE = [0, 2, 1, 4, 3, 6, 5, 8, 7, 10, 9, 12, 11, 14, 13, 16, 15, 18, 17]
LEVEL = [i for i in range(19) if VELOCITIES[i][0] == 0]
RISING = [i for i in range(19) if VELOCITIES[i][0] == 1]
FALLING = [i for i in range(19) if VELOCITIES[i][0] == -1]

EVEN_ROWS, EVEN_CLASS = (0, 7, 8, 9, 16, 17, 18), (0, 1, 3, 5, 7, 11, 15)
CROSS_ROWS = (4, 5, 6)
ODD_ROWS = ((1, 10, 11), (2, 12, 14), (3, 13, 15))
ODD_CLASS = ((1, 7, 11), (3, 7, 15), (5, 11, 15))


def moment_rows():
    c = np.array(VELOCITIES, np.float64)
    x, y, z = c[:, 0], c[:, 1], c[:, 2]
    polynomials = [
        np.ones(19), x, y, z, x * y, x * z, y * z, x**2, y**2, z**2, x * y**2, x * z**2,
        x**2 * y, x**2 * z, y * z**2, y**2 * z, x**2 * y**2, x**2 * z**2, y**2 * z**2,
    ]
    basis = []
    for row in polynomials:
        vector = row.copy()
        for earlier in basis:
            vector = vector - (vector @ earlier) / (earlier @ earlier) * earlier
        basis.append(vector)
    moments = np.stack(basis)
    return moments, np.sum(moments**2, axis=1)


MOMENTS, NORMS = moment_rows()


def kernel_entries():
    entries = {}
    for a in range(7):
        for b in range(a, 7):
            entries["even", a, b] = [
                (r, MOMENTS[r, EVEN_CLASS[a]] * MOMENTS[r, EVEN_CLASS[b]] / NORMS[r])
                for r in EVEN_ROWS
            ]
    for axis in range(3):
        for a in range(3):
            for b in range(a, 3):
                entries["odd", axis, a, b] = [
                    (
                        r,
                        MOMENTS[r, ODD_CLASS[axis][a]] * MOMENTS[r, ODD_CLASS[axis][b]] / NORMS[r],
                    )
                    for r in ODD_ROWS[axis]
                ]
    for k in range(3):
        entries["cross", k] = [(CROSS_ROWS[k], 1.0 / NORMS[CROSS_ROWS[k]])]
    return entries


ENTRIES = kernel_entries()
PLACE = {name: number for number, name in enumerate(ENTRIES)}


def fill_table(table, rates_ref):
    for name, terms in ENTRIES.items():
        total = None
        for r, factor in terms:
            if abs(factor) < 1e-12:
                continue
            term = rates_ref[r] * np.float32(factor)
            total = term if total is None else total + term
        table[PLACE[name]] = total if total is not None else jnp.float32(0.0)


def collide(f, solid, table, force):
    def even(a, b):
        return table[PLACE["even", min(a, b), max(a, b)]]

    def odd(axis, a, b):
        return table[PLACE["odd", axis, min(a, b), max(a, b)]]

    p = {i: f[i] + f[i + 1] for i in range(1, 19, 2)}
    d = {i: f[i] - f[i + 1] for i in range(1, 19, 2)}
    q_xy, q_xz, q_yz = p[7] + p[9], p[11] + p[13], p[15] + p[17]
    rho = f[0] + (p[1] + p[3] + p[5]) + (q_xy + q_xz + q_yz)
    x_parts = [d[1], d[7] + d[9], d[11] + d[13]]
    y_parts = [d[3], d[7] - d[9], d[15] + d[17]]
    z_parts = [d[5], d[11] - d[13], d[15] - d[17]]
    parts = [x_parts, y_parts, z_parts]
    j = [v[0] + v[1] + v[2] for v in parts]
    inverse = 1.0 / rho
    u = [v * inverse for v in j]
    xx, yy, zz = j[0] * u[0], j[1] * u[1], j[2] * u[2]
    square = xx + yy + zz
    third = 1.0 / 3.0
    base = rho * (1.0 / 9.0) - square * (1.0 / 6.0)
    e = [
        f[0] - (rho * third - 0.5 * square),
        p[1] - (base + 0.5 * xx),
        p[3] - (base + 0.5 * yy),
        p[5] - (base + 0.5 * zz),
        q_xy - (base + 0.5 * (xx + yy)),
        q_xz - (base + 0.5 * (xx + zz)),
        q_yz - (base + 0.5 * (yy + zz)),
    ]
    cross = [
        table[PLACE["cross", 0]] * ((p[7] - p[9]) - j[0] * u[1]),
        table[PLACE["cross", 1]] * ((p[11] - p[13]) - j[0] * u[2]),
        table[PLACE["cross", 2]] * ((p[15] - p[17]) - j[1] * u[2]),
    ]
    even_out = []
    for a in range(7):
        total = even(a, 0) * e[0]
        for b in range(1, 7):
            total = total + even(a, b) * e[b]
        even_out.append(total)
    odd_out = []
    for axis in range(3):
        share = j[axis] * third
        n = [v - share for v in parts[axis]]
        out = []
        for a in range(3):
            total = odd(axis, a, 0) * n[0] + odd(axis, a, 1) * n[1] + odd(axis, a, 2) * n[2]
            push = force[axis] * np.float32(1.0 / 6.0 if a == 0 else 1.0 / 12.0)
            out.append(push * rho - total)
        odd_out.append(out)
    (x1, x_xy, x_xz), (y1, y_xy, y_yz), (z1, z_xz, z_yz) = odd_out
    even_part = {
        1: even_out[1], 3: even_out[2], 5: even_out[3],
        7: even_out[4] + cross[0], 9: even_out[4] - cross[0],
        11: even_out[5] + cross[1], 13: even_out[5] - cross[1],
        15: even_out[6] + cross[2], 17: even_out[6] - cross[2],
    }
    odd_part = {
        1: x1, 3: y1, 5: z1, 7: x_xy + y_xy, 9: x_xy - y_xy,
        11: x_xz + z_xz, 13: x_xz - z_xz, 15: y_yz + z_yz, 17: y_yz - z_yz,
    }
    relaxed = [jnp.where(solid, f[0], f[0] - even_out[0])]
    for i in range(1, 19, 2):
        relaxed.append(jnp.where(solid, f[i + 1], (f[i] - even_part[i]) + odd_part[i]))
        relaxed.append(jnp.where(solid, f[i], (f[i + 1] - even_part[i]) - odd_part[i]))
    return relaxed


def slot(i, level, moving):
    if i in LEVEL:
        return level.at[LEVEL.index(i)]
    if i in RISING:
        return moving.at[0, RISING.index(i)]
    return moving.at[1, FALLING.index(i)]


def steps_kernel(
    pops_ref, mask_ref, rates_hbm, force_hbm, level_out, moving_out,
    rates_ref, force_ref, pops, mask, level1, send1, recv1, level2, send2, table,
    scalar_sem, pops_sem, mask_sem, send_sem, recv_sem, out_sem,
):
    count = lax.axis_size("gx")
    me = lax.axis_index("gx")
    ways = (lax.rem(me + 1, 2), lax.rem(me, 2))
    targets = (lax.rem(me + 1, count), lax.rem(me + count - 1, count))
    height, breadth = mask.shape
    chunks, groups = height // CHUNK_ROWS, height // GROUP_ROWS
    each = CHUNK_ROWS // GROUP_ROWS

    def rows(c):
        return pl.ds(pl.multiple_of(c * CHUNK_ROWS, CHUNK_ROWS), CHUNK_ROWS)

    def group_rows(g):
        return pl.ds(pl.multiple_of(g * GROUP_ROWS, GROUP_ROWS), GROUP_ROWS)

    def bring_pops(g):
        return pltpu.make_async_copy(
            pops_ref.at[:, group_rows(g), :], pops.at[:, group_rows(g), :], pops_sem.at[g]
        )

    bring_mask = pltpu.make_async_copy(mask_ref, mask, mask_sem)

    def ship(turn, way, c):
        source, target = (send1, recv1) if turn == 0 else (send2, moving_out)
        return pltpu.make_async_remote_copy(
            src_ref=source.at[way, :, rows(c), :],
            dst_ref=target.at[way, :, rows(c), :],
            send_sem=send_sem.at[turn, way, c],
            recv_sem=recv_sem.at[turn, way, c],
            device_id={"gx": lax.rem(me + 1 + way * (count - 2), count)},
            device_id_type=pl.DeviceIdType.MESH,
        )

    def put_level(c):
        return pltpu.make_async_copy(
            level2.at[:, rows(c), :], level_out.at[:, rows(c), :], out_sem.at[c]
        )

    barrier = pltpu.get_barrier_semaphore()
    for target in targets:
        pl.semaphore_signal(
            barrier, inc=1, device_id={"gx": target}, device_id_type=pl.DeviceIdType.MESH
        )
    bring_scalars = (
        pltpu.make_async_copy(rates_hbm, rates_ref, scalar_sem.at[0]),
        pltpu.make_async_copy(force_hbm, force_ref, scalar_sem.at[1]),
    )
    for bring in bring_scalars:
        bring.start()
    bring_pops(groups - 1).start()
    bring_pops(0).start()
    bring_mask.start()

    @pl.loop(1, groups - 1)
    def _(g):
        bring_pops(g).start()

    for bring in bring_scalars:
        bring.wait()
    fill_table(table, rates_ref)
    force = [force_ref[axis] for axis in range(3)]

    row = lax.broadcasted_iota(jnp.int32, (GROUP_ROWS, breadth), 0)

    def work(numbers, load, level, moving):
        for g in numbers:
            start = pl.multiple_of(g * GROUP_ROWS, GROUP_ROWS)
            here = pl.ds(start, GROUP_ROWS)
            f = [load(i, here) for i in range(19)]
            relaxed = collide(f, mask[here, :] == 1, table, force)
            for i in range(19):
                _, along_y, along_z = VELOCITIES[i]
                value, plane = relaxed[i], slot(i, level, moving)
                if along_z:
                    value = pltpu.roll(value, along_z % breadth, 1)
                if not along_y:
                    plane[here, :] = value
                    continue
                value = pltpu.roll(value, along_y % GROUP_ROWS, 0)
                beyond = lax.rem(start + (height + along_y * GROUP_ROWS), height)
                beyond = pl.ds(pl.multiple_of(beyond, GROUP_ROWS), GROUP_ROWS)
                crosses = row == (0 if along_y == 1 else GROUP_ROWS - 1)
                pltpu.store(plane.at[here, :], value, mask=jnp.logical_not(crosses))
                pltpu.store(plane.at[beyond, :], value, mask=crosses)

    bring_mask.wait()

    @pl.loop(0, chunks)
    def _(t):
        numbers = [lax.rem(t * each + (groups - 1 + k), groups) for k in range(each)]
        for g in numbers:
            bring_pops(g).wait()
        work(numbers, lambda i, here: pops[i, here, :], level1, send1)

        @pl.when(t == 0)
        def _():
            pl.semaphore_wait(barrier, 2)

        @pl.when(t >= 1)
        def _():
            for way in ways:
                ship(0, way, t - 1).start()

    for way in ways:
        ship(0, way, chunks - 1).start()

    def arrived(i, here):
        if i in LEVEL:
            return level1[LEVEL.index(i), here, :]
        return slot(i, None, recv1)[here, :]

    @pl.loop(0, chunks)
    def _(c):
        for way in range(2):
            ship(0, way, c).wait_recv()
        work([c * each + k for k in range(each)], arrived, level2, send2)

        @pl.when(c >= 2)
        def _():
            for way in ways:
                ship(1, way, c - 1).start()
            put_level(c - 1).start()

    for c in (chunks - 1, 0):
        for way in ways:
            ship(1, way, c).start()
        put_level(c).start()

    @pl.loop(0, chunks)
    def _(c):
        for way in range(2):
            ship(0, way, c).wait_send()
            ship(1, way, c).wait_send()
            ship(1, way, c).wait_recv()
        put_level(c).wait()


def place_kernel(level_ref, moving_ref, out_ref, sems):
    moves = [(moving_ref.at[0, k], out_ref.at[i]) for k, i in enumerate(RISING)]
    moves += [(moving_ref.at[1, k], out_ref.at[i]) for k, i in enumerate(FALLING)]
    first = 0
    while first < len(LEVEL):
        last = first
        while last + 1 < len(LEVEL) and LEVEL[last + 1] == LEVEL[last] + 1:
            last += 1
        size = last - first + 1
        moves.append((level_ref.at[pl.ds(first, size)], out_ref.at[pl.ds(LEVEL[first], size)]))
        first = last + 1
    copies = [
        pltpu.make_async_copy(source, target, sems.at[k])
        for k, (source, target) in enumerate(moves)
    ]
    for copy in copies:
        copy.start()
    for copy in copies:
        copy.wait()


def on_device(populations, solid_mask, relax_rates, body_force):
    channels, depth, height, breadth = populations.shape
    chunks = height // CHUNK_ROWS
    f32 = jnp.float32
    anywhere = pl.BlockSpec(memory_space=pl.ANY)
    in_hbm = pl.BlockSpec(memory_space=pltpu.HBM)
    level, moving = pl.pallas_call(
        steps_kernel,
        out_shape=(
            jax.ShapeDtypeStruct((len(LEVEL), height, breadth), f32),
            jax.ShapeDtypeStruct((2, len(RISING), height, breadth), f32),
        ),
        in_specs=[in_hbm] * 4,
        out_specs=(anywhere, anywhere),
        scratch_shapes=[
            pltpu.SMEM(relax_rates.shape, f32),
            pltpu.SMEM(body_force.shape, f32),
            pltpu.VMEM((channels, height, breadth), f32),
            pltpu.VMEM((height, breadth), jnp.int32),
            pltpu.VMEM((len(LEVEL), height, breadth), f32),
            pltpu.VMEM((2, len(RISING), height, breadth), f32),
            pltpu.VMEM((2, len(RISING), height, breadth), f32),
            pltpu.VMEM((len(LEVEL), height, breadth), f32),
            pltpu.VMEM((2, len(RISING), height, breadth), f32),
            pltpu.SMEM((len(ENTRIES),), f32),
            pltpu.SemaphoreType.DMA((2,)),
            pltpu.SemaphoreType.DMA((height // GROUP_ROWS,)),
            pltpu.SemaphoreType.DMA,
            pltpu.SemaphoreType.DMA((2, 2, chunks)),
            pltpu.SemaphoreType.DMA((2, 2, chunks)),
            pltpu.SemaphoreType.DMA((chunks,)),
        ],
        compiler_params=pltpu.CompilerParams(
            collective_id=0, has_side_effects=True, vmem_limit_bytes=32 * 1024 * 1024
        ),
    )(
        pltpu.with_memory_space_constraint(populations.reshape(channels, height, breadth), pltpu.HBM),
        pltpu.with_memory_space_constraint(solid_mask.reshape(height, breadth), pltpu.HBM),
        pltpu.with_memory_space_constraint(relax_rates, pltpu.HBM),
        pltpu.with_memory_space_constraint(body_force, pltpu.HBM),
    )
    placed = pl.pallas_call(
        place_kernel,
        out_shape=jax.ShapeDtypeStruct((channels, height, breadth), f32),
        in_specs=[anywhere, anywhere],
        out_specs=in_hbm,
        scratch_shapes=[pltpu.SemaphoreType.DMA((channels,))],
        compiler_params=pltpu.CompilerParams(vmem_limit_bytes=1024 * 1024),
    )(level, moving)
    return placed.reshape(populations.shape)


def solution(mesh):
    in_specs = (P(None, ("sample", "gx"), None, None), P(("sample", "gx"), None, None), P(), P())
    out_specs = P(None, ("sample", "gx"), None, None)
    return jax.shard_map(
        on_device, mesh=mesh, in_specs=in_specs, out_specs=out_specs, check_vma=False
    )
```
